32 devices in a mesh: wide: 4 (over y, x), narrow: 8 (over z, core).
Axes of the slice: x: 2, y: 2, z: 4, core: 2. Of those that a mesh axis runs over, the one named last changes fastest.
Arguments:
- vectors: float32 [65536, 128], P(('wide', 'narrow')), may hold values from -24 to 24
- near_blocks: bfloat16 [128, 3, 512, 512], P(('wide', 'narrow')), may hold values from -0.15625 to 0.15625
- leaf_basis: bfloat16 [65536, 256], P(('wide', 'narrow')), may hold values from -0.125 to 0.125
- transfer: bfloat16 [32, 256, 256], P(('wide', 'narrow')), may hold values from -0.125 to 0.125
- leaf_coupling: bfloat16 [32, 6, 256, 256], P(('wide', 'narrow')), may hold values from -0.15625 to 0.15625
- leaf_partners: int32 [32, 6], P(('wide', 'narrow')), may hold values from 0 to 7, as said below
- parent_coupling: bfloat16 [4, 3, 256, 256], P('wide'), may hold values from -0.21875 to 0.21875
- parent_partners: int32 [4, 3], P('wide'), may hold values from 0 to 3, as said below
- shifts: float32 [128], replicated, may hold values from -1 to 1
Outputs:
- filtered: float32 [65536, 128], P(('wide', 'narrow'))
The draws below stay inside these ranges and needn't reach their ends.
Inputs may be any that keep to these rules, and one draw needn't show every extreme that they name: `leaf_partners`: row l lists 6 different sibling indices, none equal to l mod 8. `parent_partners`: row p lists 3 different parent indices, none equal to p.
All inputs are finite; a program needn't handle non-finite values.
Results may differ from the reference program's by a relative error of at most 0.01.
Values may be sent and summed in bfloat16 or wider, within the bound.
A program may use at most 64 MiB of HBM per device.

```python
import jax
import jax.numpy as jnp
from jax import lax

NPTS_DEV = 2048
NVEC = 128
R = 256
BLK = 512
DEGREE = 3
K_LEAF = 6
K_TOP = 3
LEAVES = 32
NPTS = 65536
NBLK = 128
BLOCKS_DEV = 4
N_WIDE = 4
N_NARROW = 8


def distinct_rows(key, rows, count, picks):
    scores = jax.random.randint(key, (rows, count - 1), 0, 1 << 20) * count + jnp.arange(count - 1, dtype=jnp.int32)[None, :]
    order = jnp.argsort(scores, axis=1)
    return order[:, :picks].astype(jnp.int32)


def draw_leaf_partners(key, part):
    offsets = distinct_rows(jax.random.fold_in(key, 11), LEAVES, N_NARROW, K_LEAF)
    own = jnp.arange(LEAVES, dtype=jnp.int32) % N_NARROW
    return ((own[:, None] + 1 + offsets) % N_NARROW).astype(jnp.int32)


def draw_parent_partners(key, part):
    offsets = distinct_rows(jax.random.fold_in(key, 23), N_WIDE, N_WIDE, K_TOP)
    own = jnp.arange(N_WIDE, dtype=jnp.int32)
    return ((own[:, None] + 1 + offsets) % N_WIDE).astype(jnp.int32)


def draw_vectors(key, part):
    first = jax.random.fold_in(jax.random.fold_in(key, 37), 0)
    rise = 1.0 + 2.0 * jnp.arange(NPTS, dtype=jnp.float32) / NPTS
    base = jnp.clip(jax.random.normal(first, (NPTS, NVEC), jnp.float32), -4.0, 4.0)
    return base * rise[:, None]


def level_of(stream_key, extent, pieces, low, largest):
    loudness = 1.0
    for axis_at, shards_of in pieces:
        draws = jax.random.uniform(jax.random.fold_in(jax.random.fold_in(stream_key, 6), axis_at), (shards_of,), jnp.float32, low / len(pieces), largest / len(pieces))
        loudness = loudness * jnp.repeat(jnp.exp(draws), extent[axis_at] // shards_of).reshape((-1,) + (1,) * (len(extent) - 1 - axis_at))
    return loudness


def noise(own_key, extent, spread, most, cuts=(), kind=jnp.bfloat16):
    result = spread * jax.random.normal(own_key, extent, jnp.float32)
    if cuts:
        result = result * level_of(own_key, extent, cuts, -0.22, 0.18)
    return jnp.clip(result, -most, most).astype(kind)


def setup_inputs(seed: int = 0) -> dict:
    key_list = jax.random.split(jax.random.key(seed), 10)
    vectors = draw_vectors(jax.random.fold_in(key_list[9], 71), 0)
    near_blocks = noise(key_list[1], (NBLK, 3, BLK, BLK), (3 * BLK) ** -0.5, 0.15625, ((0, 32),))
    leaf_basis = noise(key_list[2], (NPTS, R), NPTS_DEV ** -0.5, 0.125, ((0, 32),))
    transfer = noise(key_list[3], (LEAVES, R, R), (R * N_NARROW) ** -0.5, 0.125, ((0, 32),))
    leaf_coupling = noise(key_list[4], (LEAVES, K_LEAF, R, R), (R * K_LEAF) ** -0.5, 0.15625, ((0, 32),))
    leaf_partners = draw_leaf_partners(jax.random.fold_in(key_list[9], 71), 0)
    parent_coupling = noise(key_list[6], (N_WIDE, K_TOP, R, R), (R * K_TOP) ** -0.5, 0.21875, ((0, 4),))
    parent_partners = draw_parent_partners(jax.random.fold_in(key_list[9], 71), 0)
    shifts = jnp.clip(jax.random.uniform(key_list[8], (NVEC,), jnp.float32, -1.0, 1.0), -1.0, 1.0)
    return dict(vectors=vectors, near_blocks=near_blocks, leaf_basis=leaf_basis, transfer=transfer, leaf_coupling=leaf_coupling, leaf_partners=leaf_partners, parent_coupling=parent_coupling, parent_partners=parent_partners, shifts=shifts)


def leaf_local(args):
    blocks, extended, basis, vin = args
    fields = extended.reshape(BLOCKS_DEV + 2, BLK, NVEC).astype(jnp.float32)
    wide_blocks = blocks.astype(jnp.float32)
    near = jnp.einsum('bij,bjv->biv', wide_blocks[:, 0], fields[:-2])
    near = near + jnp.einsum('bij,bjv->biv', wide_blocks[:, 1], fields[1:-1])
    near = near + jnp.einsum('bij,bjv->biv', wide_blocks[:, 2], fields[2:])
    coeff = jnp.dot(basis.T, vin, preferred_element_type=jnp.float32)
    return (near.reshape(NPTS_DEV, NVEC), coeff)

def sibling_term(args):
    coupling, picked = args
    return jnp.einsum('jrs,jsv->rv', coupling.astype(jnp.float32), picked.astype(jnp.float32))

def upward_term(args):
    matrix, coeff = args
    return jnp.dot(matrix.T, coeff, preferred_element_type=jnp.float32)

def downward_term(args):
    matrix, values = args
    return jnp.dot(matrix, values, preferred_element_type=jnp.float32)

def apply_operator(field, near_blocks, leaf_basis, transfer, leaf_coupling, leaf_partners, parent_coupling, parent_partners):
    vin = field.astype(jnp.bfloat16).reshape(LEAVES, NPTS_DEV, NVEC)
    zeros = jnp.zeros((1, BLK, NVEC), jnp.bfloat16)
    before = jnp.concatenate([zeros, vin[:-1, NPTS_DEV - BLK:]], axis=0)
    after = jnp.concatenate([vin[1:, :BLK], zeros], axis=0)
    extended = jnp.concatenate([before, vin, after], axis=1)
    blocks = near_blocks.reshape(LEAVES, BLOCKS_DEV, 3, BLK, BLK)
    basis = leaf_basis.reshape(LEAVES, NPTS_DEV, R)
    near, coeff = lax.map(leaf_local, (blocks, extended, basis, vin))
    coeff_b = coeff.astype(jnp.bfloat16)
    group = jnp.arange(LEAVES, dtype=jnp.int32) // N_NARROW
    indices = (group[:, None] * N_NARROW + leaf_partners).astype(jnp.int32)
    picked = coeff_b[indices]
    leaf_far = lax.map(sibling_term, (leaf_coupling, picked))
    upward = lax.map(upward_term, (transfer, coeff_b))
    parent_coeff = lax.optimization_barrier(jnp.sum(upward.reshape(N_WIDE, N_NARROW, R, NVEC), axis=1)).astype(jnp.bfloat16)
    top_picked = parent_coeff[parent_partners].astype(jnp.float32)
    parent_out = jnp.einsum('pjrs,pjsv->prv', parent_coupling.astype(jnp.float32), top_picked).astype(jnp.bfloat16)
    downward = lax.map(downward_term, (transfer, parent_out[group]))
    far_coeff = (leaf_far + downward).astype(jnp.bfloat16)
    far = lax.map(downward_term, (basis, far_coeff))
    return (near + far).reshape(NPTS, NVEC)

def reference(vectors, near_blocks, leaf_basis, transfer, leaf_coupling, leaf_partners, parent_coupling, parent_partners, shifts):
    operands = (near_blocks, leaf_basis, transfer, leaf_coupling, leaf_partners, parent_coupling, parent_partners)
    previous = vectors
    current = apply_operator(vectors, *operands) - shifts[None, :] * vectors
    for step in range(1, DEGREE):
        following = 2.0 * (apply_operator(current, *operands) - shifts[None, :] * current) - previous
        previous, current = (current, following)
    meansq = lax.optimization_barrier(jnp.mean(current * current, axis=0))
    return current / jnp.sqrt(meansq + 1e-06)[None, :]
```

```python
import functools

import jax
import jax.numpy as jnp
from jax import lax
from jax.experimental import pallas as pl
from jax.experimental.pallas import tpu as pltpu
from jax.sharding import PartitionSpec as P

DEGREE = 3
MESH = pl.DeviceIdType.MESH


def nn(a, b):
    return jnp.dot(a, b, preferred_element_type=jnp.float32)


def nt(a, b):
    return lax.dot_general(a, b, (((1,), (1,)), ((), ())), preferred_element_type=jnp.float32)


def tn(a, b):
    return lax.dot_general(a, b, (((0,), (0,)), ((), ())), preferred_element_type=jnp.float32)


def await_bytes(ref, sem):
    pltpu.make_async_copy(ref, ref, sem).wait()


def find(partners, count, wanted):
    slot = jnp.int32(0)
    used = jnp.int32(0)
    for j in range(count):
        hit = partners[0, j] == wanted
        slot = jnp.where(hit, j, slot)
        used = jnp.where(hit, 1, used)
    return slot, used


def masked(values, used):
    return jnp.where(used > 0, values, jnp.zeros_like(values))


def kernel(
    wides, narrows,
    vec_hbm, near_hbm, basis_hbm, transfer_hbm, leafc_hbm, topc_hbm, leafp, topp, shift_ref,
    out_hbm, scale_ref,
    t, vin, acc, near_m, basis, basis_t, transfer, leafc, topc,
    coeffs, halo, up, shares, tops, outs, squares, sq_narrow, sq_wide,
    load_sem, ag_s, ag_r, fw_s, fw_r, halo_s, halo_r, rs_s, rs_r, top_s, top_r, out_s, out_r, sq_s, sq_r,
):
    w = lax.axis_index("wide")
    n = lax.axis_index("narrow")
    leaf = w * narrows + n
    leaves = wides * narrows
    sister = n + 1 - 2 * lax.rem(n, 2)
    chips = narrows // 2
    rows, columns = vec_hbm.shape
    rank = basis.shape[1]
    blocks, _, blk, _ = near_hbm.shape
    owners, sl = up.shape[1], up.shape[2]
    own = lax.rem(n, owners)
    group = (n // owners) * owners

    def send(src, dst, ssem, rsem, wi, ni):
        copy = pltpu.make_async_remote_copy(
            src_ref=src, dst_ref=dst, send_sem=ssem, recv_sem=rsem, device_id=(wi, ni), device_id_type=MESH
        )
        copy.start()

    loads = [
        pltpu.make_async_copy(vec_hbm, t.at[0], load_sem.at[0]),
        pltpu.make_async_copy(basis_hbm, basis, load_sem.at[1]),
        pltpu.make_async_copy(transfer_hbm, transfer, load_sem.at[2]),
        pltpu.make_async_copy(near_hbm, near_m, load_sem.at[3]),
        pltpu.make_async_copy(topc_hbm, topc, load_sem.at[4]),
        pltpu.make_async_copy(leafc_hbm, leafc, load_sem.at[5]),
    ]
    for load in loads:
        load.start()

    barrier = pltpu.get_barrier_semaphore()
    for d in range(1, narrows):
        pl.semaphore_signal(barrier, inc=1, device_id=(w, lax.rem(n + d, narrows)), device_id_type=MESH)
    for d in range(1, wides):
        pl.semaphore_signal(barrier, inc=1, device_id=(lax.rem(w + d, wides), n), device_id_type=MESH)

    @pl.when(jnp.logical_and(n == 0, w > 0))
    def _():
        pl.semaphore_signal(barrier, inc=1, device_id=(w - 1, narrows - 1), device_id_type=MESH)

    @pl.when(jnp.logical_and(n == narrows - 1, w < wides - 1))
    def _():
        pl.semaphore_signal(barrier, inc=1, device_id=(w + 1, 0), device_id_type=MESH)

    t[1] = jnp.zeros((rows, columns), jnp.float32)

    @pl.when(leaf == 0)
    def _():
        for k in range(DEGREE):
            halo[k, 0] = jnp.zeros((blk, columns), jnp.bfloat16)

    @pl.when(leaf == leaves - 1)
    def _():
        for k in range(DEGREE):
            halo[k, 1] = jnp.zeros((blk, columns), jnp.bfloat16)

    loads[0].wait()
    vin[...] = t[0].astype(jnp.bfloat16)
    loads[1].wait()
    for b in range(blocks):
        at = pl.ds(b * blk, blk)
        basis_t[:, at] = basis[at, :].T
    loads[2].wait()

    before = jnp.logical_and(n == 0, w > 0).astype(jnp.int32)
    after = jnp.logical_and(n == narrows - 1, w < wides - 1).astype(jnp.int32)
    pl.semaphore_wait(barrier, narrows - 1 + wides - 1 + before + after)

    shift = shift_ref[...]

    def step(k, carry):
        cur = lax.rem(k, 2)
        nxt = 1 - cur
        coeff = nn(basis_t[...], vin[...]).astype(jnp.bfloat16)
        coeffs[k, n] = coeff
        up[k] = tn(coeff, transfer[0]).astype(jnp.bfloat16).reshape(owners, sl, rank)
        for d in range(1, narrows):
            to = lax.rem(n + d, narrows)
            send(up.at[k, lax.rem(to, owners)], shares.at[k, d - 1], rs_s.at[k], rs_r.at[k], w, to)
        for d in range(1, chips):
            to = lax.rem(n + 2 * d, narrows)
            send(coeffs.at[k, n], coeffs.at[k, n], ag_s.at[k], ag_r.at[k, d - 1], w, to)
        send(coeffs.at[k, n], coeffs.at[k, n], ag_s.at[k], fw_r.at[k], w, sister)

        @pl.when(leaf < leaves - 1)
        def _():
            to = leaf + 1
            send(
                vin.at[pl.ds(rows - blk, blk)], halo.at[k, 0], halo_s.at[k, 0], halo_r.at[k, 0],
                to // narrows, lax.rem(to, narrows),
            )

        @pl.when(leaf > 0)
        def _():
            to = leaf - 1
            send(
                vin.at[pl.ds(0, blk)], halo.at[k, 1], halo_s.at[k, 1], halo_r.at[k, 1],
                to // narrows, lax.rem(to, narrows),
            )

        @pl.when(k == 0)
        def _():
            loads[3].wait()

        def near(b):
            total = nn(near_m[b, 1], vin[b * blk : (b + 1) * blk, :])
            if b > 0:
                total += nn(near_m[b, 0], vin[(b - 1) * blk : b * blk, :])
            if b < blocks - 1:
                total += nn(near_m[b, 2], vin[(b + 1) * blk : (b + 2) * blk, :])
            acc[b * blk : (b + 1) * blk, :] = total

        for b in range(blocks // 2):
            near(b)
        await_bytes(shares.at[k], rs_r.at[k])
        total = up[k, own].astype(jnp.float32)
        for d in range(narrows - 1):
            total += shares[k, d].astype(jnp.float32)
        tops[k, w] = total.astype(jnp.bfloat16)
        for d in range(1, wides):
            send(tops.at[k, w], tops.at[k, w], top_s.at[k], top_r.at[k], lax.rem(w + d, wides), n)
        for b in range(blocks // 2, blocks):
            near(b)

        @pl.when(k == 0)
        def _():
            loads[4].wait()

        await_bytes(tops.at[k, pl.ds(0, wides - 1)], top_r.at[k])
        part = jnp.zeros((sl, rank), jnp.float32)
        for d in range(1, wides):
            at = lax.rem(w + d, wides)
            slot, used = find(topp, topc.shape[1], at)
            part += nt(masked(tops[k, at], used), topc[0, slot])
        outs[k, own] = part.astype(jnp.bfloat16)
        for d in range(1, owners):
            to = group + lax.rem(own + d, owners)
            send(outs.at[k, own], outs.at[k, own], out_s.at[k], out_r.at[k], w, to)

        for d in range(1, chips):
            at = lax.rem(n - 2 * d + narrows, narrows)
            await_bytes(coeffs.at[k, at], ag_r.at[k, d - 1])
            send(coeffs.at[k, at], coeffs.at[k, at], fw_s.at[k], fw_r.at[k], w, sister)

        @pl.when(leaf > 0)
        def _():
            await_bytes(halo.at[k, 0], halo_r.at[k, 0])

        @pl.when(leaf < leaves - 1)
        def _():
            await_bytes(halo.at[k, 1], halo_r.at[k, 1])

        acc[0:blk, :] += nn(near_m[0, 0], halo[k, 0])
        acc[rows - blk : rows, :] += nn(near_m[blocks - 1, 2], halo[k, 1])

        @pl.when(k == 0)
        def _():
            loads[5].wait()

        await_bytes(coeffs.at[k, pl.ds(0, chips)], fw_r.at[k])
        far = jnp.zeros((rank, columns), jnp.float32)
        for d in range(1, narrows):
            at = lax.rem(n + d, narrows)
            slot, used = find(leafp, leafc.shape[1], at)
            far += nn(leafc[0, slot], masked(coeffs[k, at], used))
        await_bytes(outs.at[k, pl.ds(0, owners - 1)], out_r.at[k])
        far += nt(transfer[0], outs[k].reshape(columns, rank))
        far_b = far.astype(jnp.bfloat16)

        @pl.when(leaf < leaves - 1)
        def _():
            await_bytes(halo.at[k, 0], halo_s.at[k, 0])

        @pl.when(leaf > 0)
        def _():
            await_bytes(halo.at[k, 1], halo_s.at[k, 1])

        factor = jnp.where(k == 0, 1.0, 2.0)
        sums = jnp.zeros((8, columns), jnp.float32)
        for b in range(blocks):
            at = pl.ds(b * blk, blk)
            applied = acc[at, :] + nn(basis[at, :], far_b)
            fresh = factor * (applied - shift * t[cur, at, :]) - t[nxt, at, :]
            t[nxt, at, :] = fresh
            vin[at, :] = fresh.astype(jnp.bfloat16)
            sums += jnp.sum((fresh * fresh).reshape(blk // 8, 8, columns), axis=0)
        squares[0] = sums
        return carry

    lax.fori_loop(0, DEGREE, step, 0)

    result = pltpu.make_async_copy(t.at[DEGREE % 2], out_hbm, load_sem.at[6])
    result.start()
    for d in range(1, narrows):
        send(squares.at[0], sq_narrow.at[d - 1], sq_s.at[0], sq_r.at[0], w, lax.rem(n + d, narrows))
    await_bytes(sq_narrow, sq_r.at[0])
    total = squares[0]
    for d in range(narrows - 1):
        total += sq_narrow[d]
    squares[1] = total
    for d in range(1, wides):
        send(squares.at[1], sq_wide.at[d - 1], sq_s.at[1], sq_r.at[1], lax.rem(w + d, wides), n)

    for k in range(DEGREE):
        await_bytes(shares.at[k], rs_s.at[k])
        await_bytes(coeffs.at[k, pl.ds(0, chips)], ag_s.at[k])
        await_bytes(coeffs.at[k, pl.ds(0, chips - 1)], fw_s.at[k])
        await_bytes(tops.at[k, pl.ds(0, wides - 1)], top_s.at[k])
        await_bytes(outs.at[k, pl.ds(0, owners - 1)], out_s.at[k])
    await_bytes(sq_narrow, sq_s.at[0])
    await_bytes(sq_wide, sq_r.at[1])
    for d in range(wides - 1):
        total += sq_wide[d]
    mean = jnp.sum(total, axis=0, keepdims=True) / (rows * leaves)
    scale_ref[...] = jnp.sqrt(mean + 1e-06)
    await_bytes(sq_wide, sq_s.at[1])
    result.wait()


def shards(wides, narrows, vectors, near_blocks, leaf_basis, transfer, leaf_coupling, leaf_partners, parent_coupling, parent_partners, shifts):
    rows, columns = vectors.shape
    rank = leaf_basis.shape[1]
    blk = near_blocks.shape[2]
    sl = max(16, columns // narrows)
    owners = columns // sl
    bf16, f32 = jnp.bfloat16, jnp.float32
    dma = pltpu.SemaphoreType.DMA
    anywhere = pl.BlockSpec(memory_space=pl.ANY)
    scalars = pl.BlockSpec(memory_space=pltpu.SMEM)
    local = pl.BlockSpec(memory_space=pltpu.VMEM)
    raw, scale = pl.pallas_call(
        functools.partial(kernel, wides, narrows),
        out_shape=(
            jax.ShapeDtypeStruct((rows, columns), f32),
            jax.ShapeDtypeStruct((1, columns), f32),
        ),
        in_specs=[anywhere] * 6 + [scalars] * 2 + [local],
        out_specs=(anywhere, local),
        scratch_shapes=[
            pltpu.VMEM((2, rows, columns), f32),
            pltpu.VMEM((rows, columns), bf16),
            pltpu.VMEM((rows, columns), f32),
            pltpu.VMEM(near_blocks.shape, bf16),
            pltpu.VMEM((rows, rank), bf16),
            pltpu.VMEM((rank, rows), bf16),
            pltpu.VMEM(transfer.shape, bf16),
            pltpu.VMEM(leaf_coupling.shape, bf16),
            pltpu.VMEM(parent_coupling.shape, bf16),
            pltpu.VMEM((DEGREE, narrows, rank, columns), bf16),
            pltpu.VMEM((DEGREE, 2, blk, columns), bf16),
            pltpu.VMEM((DEGREE, owners, sl, rank), bf16),
            pltpu.VMEM((DEGREE, narrows - 1, sl, rank), bf16),
            pltpu.VMEM((DEGREE, wides, sl, rank), bf16),
            pltpu.VMEM((DEGREE, owners, sl, rank), bf16),
            pltpu.VMEM((2, 8, columns), f32),
            pltpu.VMEM((narrows - 1, 8, columns), f32),
            pltpu.VMEM((wides - 1, 8, columns), f32),
            dma((7,)),
            dma((DEGREE,)), dma((DEGREE, narrows // 2)),
            dma((DEGREE,)), dma((DEGREE,)),
            dma((DEGREE, 2)), dma((DEGREE, 2)),
            dma((DEGREE,)), dma((DEGREE,)),
            dma((DEGREE,)), dma((DEGREE,)),
            dma((DEGREE,)), dma((DEGREE,)),
            dma((2,)), dma((2,)),
        ],
        compiler_params=pltpu.CompilerParams(
            collective_id=0, has_side_effects=True, vmem_limit_bytes=56 * 1024 * 1024
        ),
    )(
        vectors, near_blocks, leaf_basis, transfer, leaf_coupling, parent_coupling,
        leaf_partners, parent_partners, shifts[None, :],
    )
    return raw / scale


def solution(mesh):
    return jax.shard_map(
        functools.partial(shards, mesh.shape["wide"], mesh.shape["narrow"]),
        mesh=mesh,
        in_specs=(
            P(("wide", "narrow"), None),
            P(("wide", "narrow"), None, None, None),
            P(("wide", "narrow"), None),
            P(("wide", "narrow"), None, None),
            P(("wide", "narrow"), None, None, None),
            P(("wide", "narrow"), None),
            P("wide", None, None, None),
            P("wide", None),
            P(),
        ),
        out_specs=P(("wide", "narrow"), None),
        check_vma=False,
    )
```

```python
import functools

import jax
import jax.numpy as jnp
from jax import lax
from jax.experimental import pallas as pl
from jax.experimental.pallas import tpu as pltpu
from jax.sharding import PartitionSpec as P

DEGREE = 3
MESH = pl.DeviceIdType.MESH


def nn(a, b):
    return jnp.dot(a, b, preferred_element_type=jnp.float32)


def nt(a, b):
    return lax.dot_general(a, b, (((1,), (1,)), ((), ())), preferred_element_type=jnp.float32)


def tn(a, b):
    return lax.dot_general(a, b, (((0,), (0,)), ((), ())), preferred_element_type=jnp.float32)


def await_bytes(ref, sem):
    pltpu.make_async_copy(ref, ref, sem).wait()


def find(partners, count, wanted):
    slot = jnp.int32(0)
    used = jnp.int32(0)
    for j in range(count):
        hit = partners[0, j] == wanted
        slot = jnp.where(hit, j, slot)
        used = jnp.where(hit, 1, used)
    return slot, used


def masked(values, used):
    return jnp.where(used > 0, values, jnp.zeros_like(values))


def kernel(
    wides, narrows,
    vec_hbm, near_hbm, basis_hbm, transfer_hbm, leafc_hbm, topc_hbm, leafp, topp, shift_ref,
    out_hbm, scale_ref,
    t, vin, acc, near_m, basis, basis_t, gram, transfer, leafc, topc,
    coeffs, halo, up, shares, tops, outs, squares, sq_narrow, sq_wide,
    load_sem, ag_s, ag_r, fw_s, fw_r, halo_s, halo_r, rs_s, rs_r, top_s, top_r, out_s, out_r, sq_s, sq_r,
):
    w = lax.axis_index("wide")
    n = lax.axis_index("narrow")
    leaf = w * narrows + n
    leaves = wides * narrows
    sister = n + 1 - 2 * lax.rem(n, 2)
    chips = narrows // 2
    rows, columns = vec_hbm.shape
    rank = basis.shape[1]
    blocks, _, blk, _ = near_hbm.shape
    owners, sl = up.shape[1], up.shape[2]
    own = lax.rem(n, owners)
    group = (n // owners) * owners

    def send(src, dst, ssem, rsem, wi, ni):
        copy = pltpu.make_async_remote_copy(
            src_ref=src, dst_ref=dst, send_sem=ssem, recv_sem=rsem, device_id=(wi, ni), device_id_type=MESH
        )
        copy.start()

    loads = [
        pltpu.make_async_copy(vec_hbm, t.at[0], load_sem.at[0]),
        pltpu.make_async_copy(basis_hbm, basis, load_sem.at[1]),
        pltpu.make_async_copy(transfer_hbm, transfer, load_sem.at[2]),
        pltpu.make_async_copy(near_hbm, near_m, load_sem.at[3]),
        pltpu.make_async_copy(topc_hbm, topc, load_sem.at[4]),
        pltpu.make_async_copy(leafc_hbm, leafc, load_sem.at[5]),
    ]
    for load in loads:
        load.start()

    barrier = pltpu.get_barrier_semaphore()
    for d in range(1, narrows):
        pl.semaphore_signal(barrier, inc=1, device_id=(w, lax.rem(n + d, narrows)), device_id_type=MESH)
    for d in range(1, wides):
        pl.semaphore_signal(barrier, inc=1, device_id=(lax.rem(w + d, wides), n), device_id_type=MESH)

    @pl.when(jnp.logical_and(n == 0, w > 0))
    def _():
        pl.semaphore_signal(barrier, inc=1, device_id=(w - 1, narrows - 1), device_id_type=MESH)

    @pl.when(jnp.logical_and(n == narrows - 1, w < wides - 1))
    def _():
        pl.semaphore_signal(barrier, inc=1, device_id=(w + 1, 0), device_id_type=MESH)

    @pl.when(leaf == 0)
    def _():
        for k in range(DEGREE):
            halo[k, 0] = jnp.zeros((blk, columns), jnp.bfloat16)

    @pl.when(leaf == leaves - 1)
    def _():
        for k in range(DEGREE):
            halo[k, 1] = jnp.zeros((blk, columns), jnp.bfloat16)

    loads[0].wait()
    vin[...] = t[0].astype(jnp.bfloat16)
    loads[1].wait()
    for b in range(blocks):
        at = pl.ds(b * blk, blk)
        basis_t[:, at] = basis[at, :].T
    loads[2].wait()

    before = jnp.logical_and(n == 0, w > 0).astype(jnp.int32)
    after = jnp.logical_and(n == narrows - 1, w < wides - 1).astype(jnp.int32)
    pl.semaphore_wait(barrier, narrows - 1 + wides - 1 + before + after)

    shift = shift_ref[...]

    def update(k, far_b):
        sums = jnp.zeros((8, columns), jnp.float32)
        for b in range(blocks):
            at = pl.ds(b * blk, blk)
            fresh = acc[at, :] + (1.0 if k == 1 else 2.0) * nn(basis[at, :], far_b)
            t[k % 2, at, :] = fresh
            if k < DEGREE:
                vin[at, :] = fresh.astype(jnp.bfloat16)
            else:
                sums += jnp.sum((fresh * fresh).reshape(blk // 8, 8, columns), axis=0)
        return sums

    coeff = nn(basis_t[...], vin[...]).astype(jnp.bfloat16)
    far_b = None
    for k in range(DEGREE):
        coeffs[k, n] = coeff
        up[k] = tn(coeff, transfer[0]).astype(jnp.bfloat16).reshape(owners, sl, rank)
        for d in range(1, narrows):
            to = lax.rem(n + d, narrows)
            send(up.at[k, lax.rem(to, owners)], shares.at[k, d - 1], rs_s.at[k], rs_r.at[k], w, to)
        for d in range(1, chips):
            to = lax.rem(n + 2 * d, narrows)
            send(coeffs.at[k, n], coeffs.at[k, n], ag_s.at[k], ag_r.at[k, d - 1], w, to)
        send(coeffs.at[k, n], coeffs.at[k, n], ag_s.at[k], fw_r.at[k], w, sister)
        if k > 0:
            update(k, far_b)

        @pl.when(leaf < leaves - 1)
        def _():
            to = leaf + 1
            send(
                vin.at[pl.ds(rows - blk, blk)], halo.at[k, 0], halo_s.at[k, 0], halo_r.at[k, 0],
                to // narrows, lax.rem(to, narrows),
            )

        @pl.when(leaf > 0)
        def _():
            to = leaf - 1
            send(
                vin.at[pl.ds(0, blk)], halo.at[k, 1], halo_s.at[k, 1], halo_r.at[k, 1],
                to // narrows, lax.rem(to, narrows),
            )

        if k == 0:
            gram[...] = nn(basis_t[...], basis[...]).astype(jnp.bfloat16)
            loads[3].wait()

        def near(b):
            total = nn(near_m[b, 1], vin[b * blk : (b + 1) * blk, :])
            if b > 0:
                total += nn(near_m[b, 0], vin[(b - 1) * blk : b * blk, :])
            if b < blocks - 1:
                total += nn(near_m[b, 2], vin[(b + 1) * blk : (b + 2) * blk, :])
            acc[b * blk : (b + 1) * blk, :] = total

        for b in range(blocks // 2):
            near(b)
        await_bytes(shares.at[k], rs_r.at[k])
        total = up[k, own].astype(jnp.float32)
        for d in range(narrows - 1):
            total += shares[k, d].astype(jnp.float32)
        tops[k, w] = total.astype(jnp.bfloat16)
        for d in range(1, wides):
            send(tops.at[k, w], tops.at[k, w], top_s.at[k], top_r.at[k], lax.rem(w + d, wides), n)
        for b in range(blocks // 2, blocks):
            near(b)

        if k == 0:
            loads[4].wait()

        await_bytes(tops.at[k, pl.ds(0, wides - 1)], top_r.at[k])
        part = jnp.zeros((sl, rank), jnp.float32)
        for d in range(1, wides):
            at = lax.rem(w + d, wides)
            slot, used = find(topp, topc.shape[1], at)
            part += nt(masked(tops[k, at], used), topc[0, slot])
        outs[k, own] = part.astype(jnp.bfloat16)
        for d in range(1, owners):
            to = group + lax.rem(own + d, owners)
            send(outs.at[k, own], outs.at[k, own], out_s.at[k], out_r.at[k], w, to)

        for d in range(1, chips):
            at = lax.rem(n - 2 * d + narrows, narrows)
            await_bytes(coeffs.at[k, at], ag_r.at[k, d - 1])
            send(coeffs.at[k, at], coeffs.at[k, at], fw_s.at[k], fw_r.at[k], w, sister)

        @pl.when(leaf > 0)
        def _():
            await_bytes(halo.at[k, 0], halo_r.at[k, 0])

        @pl.when(leaf < leaves - 1)
        def _():
            await_bytes(halo.at[k, 1], halo_r.at[k, 1])

        acc[0:blk, :] += nn(near_m[0, 0], halo[k, 0])
        acc[rows - blk : rows, :] += nn(near_m[blocks - 1, 2], halo[k, 1])
        local = jnp.zeros((rank, columns), jnp.float32)
        for b in range(blocks):
            at = pl.ds(b * blk, blk)
            base = acc[at, :] - shift * t[k % 2, at, :]
            if k > 0:
                base = 2.0 * base - t[1 - k % 2, at, :]
            acc[at, :] = base
            if k < DEGREE - 1:
                local += nn(basis_t[:, at], base.astype(jnp.bfloat16))

        if k == 0:
            loads[5].wait()

        await_bytes(coeffs.at[k, pl.ds(0, chips)], fw_r.at[k])
        far = jnp.zeros((rank, columns), jnp.float32)
        for d in range(1, narrows):
            at = lax.rem(n + d, narrows)
            slot, used = find(leafp, leafc.shape[1], at)
            far += nn(leafc[0, slot], masked(coeffs[k, at], used))
        await_bytes(outs.at[k, pl.ds(0, owners - 1)], out_r.at[k])
        far += nt(transfer[0], outs[k].reshape(columns, rank))
        far_b = far.astype(jnp.bfloat16)

        @pl.when(leaf < leaves - 1)
        def _():
            await_bytes(halo.at[k, 0], halo_s.at[k, 0])

        @pl.when(leaf > 0)
        def _():
            await_bytes(halo.at[k, 1], halo_s.at[k, 1])

        if k < DEGREE - 1:
            coeff = (local + (1.0 if k == 0 else 2.0) * nn(gram[...], far_b)).astype(jnp.bfloat16)

    squares[0] = update(DEGREE, far_b)
    result = pltpu.make_async_copy(t.at[DEGREE % 2], out_hbm, load_sem.at[6])
    result.start()
    for d in range(1, narrows):
        send(squares.at[0], sq_narrow.at[d - 1], sq_s.at[0], sq_r.at[0], w, lax.rem(n + d, narrows))
    await_bytes(sq_narrow, sq_r.at[0])
    total = squares[0]
    for d in range(narrows - 1):
        total += sq_narrow[d]
    squares[1] = total
    for d in range(1, wides):
        send(squares.at[1], sq_wide.at[d - 1], sq_s.at[1], sq_r.at[1], lax.rem(w + d, wides), n)

    for k in range(DEGREE):
        await_bytes(shares.at[k], rs_s.at[k])
        await_bytes(coeffs.at[k, pl.ds(0, chips)], ag_s.at[k])
        await_bytes(coeffs.at[k, pl.ds(0, chips - 1)], fw_s.at[k])
        await_bytes(tops.at[k, pl.ds(0, wides - 1)], top_s.at[k])
        await_bytes(outs.at[k, pl.ds(0, owners - 1)], out_s.at[k])
    await_bytes(sq_narrow, sq_s.at[0])
    await_bytes(sq_wide, sq_r.at[1])
    for d in range(wides - 1):
        total += sq_wide[d]
    mean = jnp.sum(total, axis=0, keepdims=True) / (rows * leaves)
    scale_ref[...] = jnp.sqrt(mean + 1e-06)
    await_bytes(sq_wide, sq_s.at[1])
    result.wait()


def shards(wides, narrows, vectors, near_blocks, leaf_basis, transfer, leaf_coupling, leaf_partners, parent_coupling, parent_partners, shifts):
    rows, columns = vectors.shape
    rank = leaf_basis.shape[1]
    blk = near_blocks.shape[2]
    sl = max(16, columns // narrows)
    owners = columns // sl
    bf16, f32 = jnp.bfloat16, jnp.float32
    dma = pltpu.SemaphoreType.DMA
    anywhere = pl.BlockSpec(memory_space=pl.ANY)
    scalars = pl.BlockSpec(memory_space=pltpu.SMEM)
    local = pl.BlockSpec(memory_space=pltpu.VMEM)
    raw, scale = pl.pallas_call(
        functools.partial(kernel, wides, narrows),
        out_shape=(
            jax.ShapeDtypeStruct((rows, columns), f32),
            jax.ShapeDtypeStruct((1, columns), f32),
        ),
        in_specs=[anywhere] * 6 + [scalars] * 2 + [local],
        out_specs=(anywhere, local),
        scratch_shapes=[
            pltpu.VMEM((2, rows, columns), f32),
            pltpu.VMEM((rows, columns), bf16),
            pltpu.VMEM((rows, columns), f32),
            pltpu.VMEM(near_blocks.shape, bf16),
            pltpu.VMEM((rows, rank), bf16),
            pltpu.VMEM((rank, rows), bf16),
            pltpu.VMEM((rank, rank), bf16),
            pltpu.VMEM(transfer.shape, bf16),
            pltpu.VMEM(leaf_coupling.shape, bf16),
            pltpu.VMEM(parent_coupling.shape, bf16),
            pltpu.VMEM((DEGREE, narrows, rank, columns), bf16),
            pltpu.VMEM((DEGREE, 2, blk, columns), bf16),
            pltpu.VMEM((DEGREE, owners, sl, rank), bf16),
            pltpu.VMEM((DEGREE, narrows - 1, sl, rank), bf16),
            pltpu.VMEM((DEGREE, wides, sl, rank), bf16),
            pltpu.VMEM((DEGREE, owners, sl, rank), bf16),
            pltpu.VMEM((2, 8, columns), f32),
            pltpu.VMEM((narrows - 1, 8, columns), f32),
            pltpu.VMEM((wides - 1, 8, columns), f32),
            dma((7,)),
            dma((DEGREE,)), dma((DEGREE, narrows // 2)),
            dma((DEGREE,)), dma((DEGREE,)),
            dma((DEGREE, 2)), dma((DEGREE, 2)),
            dma((DEGREE,)), dma((DEGREE,)),
            dma((DEGREE,)), dma((DEGREE,)),
            dma((DEGREE,)), dma((DEGREE,)),
            dma((2,)), dma((2,)),
        ],
        compiler_params=pltpu.CompilerParams(
            collective_id=0, has_side_effects=True, vmem_limit_bytes=56 * 1024 * 1024
        ),
    )(
        vectors, near_blocks, leaf_basis, transfer, leaf_coupling, parent_coupling,
        leaf_partners, parent_partners, shifts[None, :],
    )
    return raw / scale


def solution(mesh):
    return jax.shard_map(
        functools.partial(shards, mesh.shape["wide"], mesh.shape["narrow"]),
        mesh=mesh,
        in_specs=(
            P(("wide", "narrow"), None),
            P(("wide", "narrow"), None, None, None),
            P(("wide", "narrow"), None),
            P(("wide", "narrow"), None, None),
            P(("wide", "narrow"), None, None, None),
            P(("wide", "narrow"), None),
            P("wide", None, None, None),
            P("wide", None),
            P(),
        ),
        out_specs=P(("wide", "narrow"), None),
        check_vma=False,
    )
```
